256 devices in a mesh: dp: 64 (over z, y, core), mp: 4 (over x).
Axes of the slice: x: 4, y: 4, z: 8, core: 2. Of those that a mesh axis runs over, the one named last changes fastest.
Arguments:
- queries: bfloat16 [32768, 8192], P('dp', 'mp'), may hold values from -64 to 64
- comp_keys: bfloat16 [32768, 1024], P('dp', 'mp'), may hold values from -12 to 12
- comp_values: bfloat16 [32768, 1024], P('dp', 'mp'), may hold values from -6 to 6
- prefix_keys: bfloat16 [131072, 1024], P(('dp', 'mp')), may hold values from -6 to 6
- prefix_values: bfloat16 [131072, 1024], P(('dp', 'mp')), may hold values from -6 to 6
- prompt_of: int32 [2048, 1], P('dp'), may hold values from 0 to 63; in each aligned block of 32 rows (0 to 31, 32 to 63, ...) no two rows name the same one
Outputs:
- attended: bfloat16 [32768, 8192], P('dp', 'mp')
The draws below stay inside these ranges and needn't reach their ends.
Inputs may be any that keep to these rules, and one draw needn't show every extreme that they name: `prompt_of`: among the 32 completions of one device, at most 1 name the same prompt.
All inputs are finite; a program needn't handle non-finite values.
Results may differ from the reference program's by a relative error of at most 0.0051.
Values may be sent and summed in bfloat16 or wider, within the bound.
A program may use at most 128 MiB of HBM per device.

```python
import math
import jax
import jax.numpy as jnp
import numpy as np
from jax import lax

HQ = 64
HK = 8
HD = 128
LEN = 16
PREF = 2048
COMP_DEV = 32
PROMPTS = 64
CAP = 1
COMPS = 2048
ROWS = 32768


def draw_queries(key, part):
    key = jax.random.fold_in(key, 11)
    shape = (ROWS, HQ * HD)
    return jnp.clip(jax.random.normal(key, shape, jnp.float32), -6.0, 6.0).astype(jnp.bfloat16)


def draw_comp_keys(key, part):
    key = jax.random.fold_in(key, 23)
    shape = (ROWS, HK * HD)
    return jnp.clip(2.0 * jax.random.normal(key, shape, jnp.float32), -12.0, 12.0).astype(jnp.bfloat16)


def draw_prefix_keys(key, part):
    key = jax.random.fold_in(key, 37)
    shape = (PROMPTS * PREF, HK * HD)
    return jnp.clip(jax.random.normal(key, shape, jnp.float32), -6.0, 6.0).astype(jnp.bfloat16)


def block_levels(key, dims, cuts, low, top_value):
    factor_of = 1.0
    for axis_at, parts in cuts:
        heights = jax.random.uniform(jax.random.fold_in(jax.random.fold_in(key, 6), axis_at), (parts,), jnp.float32, low / len(cuts), top_value / len(cuts))
        factor_of = factor_of * jnp.repeat(jnp.exp(heights), dims[axis_at] // parts).reshape((-1,) + (1,) * (len(dims) - 1 - axis_at))
    return factor_of


def shared_out(own_key, own, number, rows, number_of, top, reach, skew):
    ranking = jax.random.permutation(own_key, number_of)
    heavy_load, ordinary = shares(number_of, rows * top, reach, skew, True), shares(number_of, rows * top, reach, skew, False)
    places = jnp.arange(number_of)

    def named(sizes, rotation):
        used = int((sizes > 0).sum())
        fixed = max(1, used // 4)
        shifted = fixed + (places - fixed + rotation * (used - fixed)) % max(1, number_of - fixed)
        return jnp.zeros((number_of,), jnp.int32).at[ranking[jnp.where(places < fixed, places, shifted)]].set(jnp.asarray(sizes, jnp.int32))

    sizes = jnp.where(number % 4 == 0, named(heavy_load, number // 4), named(ordinary, number - number // 4 - 1))
    mixed = jax.random.permutation(jax.random.fold_in(own, 3), number_of)
    giver, receiver = mixed[0:number_of // 2 * 2:2], mixed[1:number_of // 2 * 2:2]
    margin = jnp.minimum(sizes[giver] - 1, reach - sizes[receiver]) // 2
    margin = jnp.where((giver == ranking[0]) | (receiver == ranking[0]) | (sizes[receiver] == 0), 0, jnp.maximum(margin, 0))
    shifted = jax.random.randint(jax.random.fold_in(own, 4), (number_of // 2,), 0, 1 << 20) % (margin + 1)
    sizes = sizes.at[giver].add(-shifted).at[receiver].add(shifted)
    members = jnp.searchsorted(jnp.cumsum(sizes), jnp.arange(rows * top), side="right").astype(jnp.int32)
    listing = members.reshape(top, rows).T
    listing = listing[jax.random.permutation(jax.random.fold_in(own, 1), rows)]
    rotation = jax.random.randint(jax.random.fold_in(own, 2), (rows, 1), 0, top)
    return jnp.take_along_axis(listing, (jnp.arange(top)[None, :] + rotation) % top, axis=1)


def shares(amount, total, bound, slope, full):
    portions = [(1 << 20) // math.isqrt(grade ** slope) + 1 for grade in range(1, amount + 1)]
    largest = bound if full else min(bound, max(-(-total // amount), total * portions[0] // sum(portions)))
    least = 1 if total - largest >= amount - 1 else 0
    given, spare = [largest] + [least] * (amount - 1), total - largest - least * (amount - 1)
    while spare > 0:
        free = [i for i in range(1, amount) if given[i] < largest] or [i for i in range(1, amount) if given[i] < bound]
        pool, left = sum([portions[i] for i in free]), spare
        for i in free:
            more = min(bound - given[i], max(1, left * portions[i] // pool), spare)
            given[i] = given[i] + more
            spare = spare - more
    return np.array(given)


def bell_draw(key, shape, scale, limit, split=(), kind=jnp.bfloat16):
    drawn = scale * jax.random.normal(key, shape, jnp.float32)
    if split:
        drawn = drawn * block_levels(key, shape, split, -0.22, 0.18)
    return jnp.clip(drawn, -limit, limit).astype(kind)


def setup_inputs(seed: int = 0) -> dict:
    arg_keys = jax.random.split(jax.random.key(seed), 7)
    queries = draw_queries(jax.random.fold_in(arg_keys[6], 71), 0)
    comp_keys = draw_comp_keys(jax.random.fold_in(arg_keys[6], 71), 0)
    comp_values = bell_draw(arg_keys[2], (ROWS, HK * HD), 1.0, 6.0, ((0, 64), (1, 4)))
    prefix_keys = draw_prefix_keys(jax.random.fold_in(arg_keys[6], 71), 0)
    prefix_values = bell_draw(arg_keys[4], (PROMPTS * PREF, HK * HD), 1.0, 6.0, ((0, 256),))
    prompt_of_keys = jax.random.split(jax.random.fold_in(arg_keys[5], 1), COMPS // COMP_DEV)
    prompt_of_turns = jax.random.permutation(jax.random.fold_in(arg_keys[5], 3), COMPS // COMP_DEV)
    prompt_of = jax.vmap(lambda own, number: shared_out(jax.random.fold_in(arg_keys[5], 2), own, number, COMP_DEV, PROMPTS, 1, CAP, 2))(prompt_of_keys, prompt_of_turns).reshape((COMPS, 1))
    return {"queries": queries, "comp_keys": comp_keys, "comp_values": comp_values, "prefix_keys": prefix_keys, "prefix_values": prefix_values, "prompt_of": prompt_of}


def reference(queries, comp_keys, comp_values, prefix_keys, prefix_values, prompt_of):
    group_size = HQ // HK
    score_scale = 1.0 / math.sqrt(HD)
    query_rows = queries.reshape(COMPS, LEN, HK, group_size, HD)
    comp_k = comp_keys.reshape(COMPS, LEN, HK, HD)
    comp_v = comp_values.reshape(COMPS, LEN, HK, HD)
    prompt_keys = prefix_keys.reshape(PROMPTS, PREF, HK, HD)
    prompt_values = prefix_values.reshape(PROMPTS, PREF, HK, HD)
    owners = prompt_of[:, 0].astype(jnp.int32)
    causal = jnp.arange(LEN)[:, None] >= jnp.arange(LEN)[None, :]

    def attend_one(inputs):
        rows_q, rows_k, rows_v, prompt = inputs
        cache_k = lax.dynamic_index_in_dim(prompt_keys, prompt, 0, keepdims=False).astype(jnp.float32)
        cache_v = lax.dynamic_index_in_dim(prompt_values, prompt, 0, keepdims=False).astype(jnp.float32)
        query_f = rows_q.astype(jnp.float32)
        scores = jnp.einsum('lkgd,pkd->lkgp', query_f, cache_k) * score_scale
        prefix_max = lax.optimization_barrier(jnp.max(scores, axis=-1, keepdims=True))
        prefix_exp = jnp.exp(scores - prefix_max)
        prefix_total = lax.optimization_barrier(jnp.sum(prefix_exp, axis=-1, keepdims=True))
        prefix_weights = prefix_exp.astype(jnp.bfloat16).astype(jnp.float32)
        prefix_sum = jnp.einsum('lkgp,pkd->lkgd', prefix_weights, cache_v)
        prefix_mixed = (prefix_sum / prefix_total).astype(jnp.bfloat16).astype(jnp.float32)
        prefix_lse = prefix_max[..., 0] + jnp.log(prefix_total[..., 0])
        own_scores = jnp.einsum('lkgd,mkd->lkgm', query_f, rows_k.astype(jnp.float32)) * score_scale
        own_scores = jnp.where(causal[:, None, None, :], own_scores, -1e+30)
        own_max = lax.optimization_barrier(jnp.max(own_scores, axis=-1, keepdims=True))
        own_exp = jnp.exp(own_scores - own_max)
        own_total = lax.optimization_barrier(jnp.sum(own_exp, axis=-1, keepdims=True))
        own_weights = own_exp.astype(jnp.bfloat16).astype(jnp.float32)
        own_sum = jnp.einsum('lkgm,mkd->lkgd', own_weights, rows_v.astype(jnp.float32))
        own_mixed = own_sum / own_total
        own_lse = own_max[..., 0] + jnp.log(own_total[..., 0])
        ceiling = jnp.maximum(prefix_lse, own_lse)
        far_weight = jnp.exp(prefix_lse - ceiling)
        near_weight = jnp.exp(own_lse - ceiling)
        blended = (prefix_mixed * far_weight[..., None] + own_mixed * near_weight[..., None]) / (far_weight + near_weight)[..., None]
        return blended.astype(jnp.bfloat16)
    attended = lax.map(attend_one, (query_rows, comp_k, comp_v, owners), batch_size=8)
    return attended.reshape(ROWS, HQ * HD)
```

```python
import functools
import math

import jax
import jax.numpy as jnp
from jax import lax
from jax.experimental import pallas as pl
from jax.experimental.pallas import tpu as pltpu
from jax.sharding import PartitionSpec as P

MESH = pl.DeviceIdType.MESH
HD = 128
LEN = 16
GROUP = 8
HEADS = 2
PLANE = 8
RING = 8
SLOT = GROUP * HD
WIDE = SLOT + HD
SCALE = 1.0 / math.sqrt(HD)
LOG2E = math.log2(math.e)
ORDER = (0, 1, 7, 2, 6, 3, 5, 4)


def split3(x):
    hi = x.astype(jnp.bfloat16)
    rest = x - hi.astype(jnp.float32)
    mid = rest.astype(jnp.bfloat16)
    low = (rest - mid.astype(jnp.float32)).astype(jnp.bfloat16)
    return hi, mid, low


def by_group(column):
    lane = lax.broadcasted_iota(jnp.int32, (LEN, HD), 1)
    out = jnp.zeros((LEN, HD), jnp.float32)
    for g in range(GROUP):
        out = jnp.where(lane == g, column[g * LEN : (g + 1) * LEN], out)
    return out


def rows_of(slot):
    return [slot[:, g * HD : (g + 1) * HD] for g in range(GROUP)]


def kernel(
    idx, pos, q, ck, cv, pk, pv, out,
    cache, qs, fs, nq, relay_q, fq, no, fo, relay_o, ret, own, own_lse,
    send_sem, recv_sem, local_sem,
):
    dp, x = lax.axis_index("dp"), lax.axis_index("mp")
    z, lane = dp // PLANE, dp % PLANE
    xs = lax.axis_size("mp")
    share = pk.shape[0]
    comps = q.shape[0]

    def to_x(e):
        return (dp, (x + e) % xs)

    def to_z(k):
        return (((z + k + RING) % RING) * PLANE + lane, x)

    def to_lane(d):
        return (z * PLANE + (lane + d + PLANE) % PLANE, x)

    barrier = pltpu.get_barrier_semaphore()
    friends = (
        [to_x(e) for e in range(1, xs)]
        + [to_z(k) for k in (1, -1, 2, -2)]
        + [to_lane(d) for d in range(1, PLANE)]
    )
    for friend in friends:
        pl.semaphore_signal(barrier, 1, device_id=friend, device_id_type=MESH)
    pl.semaphore_wait(barrier, len(friends))

    count = [0]
    sent = []

    def remote(src, dst, device):
        n = count[0]
        count[0] += 1
        copy = pltpu.make_async_remote_copy(
            src_ref=src, dst_ref=dst, send_sem=send_sem.at[n], recv_sem=recv_sem.at[n],
            device_id=device, device_id_type=MESH,
        )
        copy.start()
        sent.append(copy)
        return copy

    def columns(e, h):
        return pl.ds(pl.multiple_of(((x + e) % xs) * (HEADS * HD) + h * HD, HD), HD)

    def exchange(h):
        copies = []
        for w, whole in enumerate((pk, pv)):
            mine = pltpu.make_async_copy(
                whole.at[:, columns(0, h)], cache.at[0, h, w, pl.ds(0, share)],
                local_sem.at[h * 2 + w],
            )
            mine.start()
            copies.append([mine] + [
                remote(whole.at[:, columns(e, h)], cache.at[0, h, w, pl.ds(e * share, share)], to_x(e))
                for e in range(1, xs)
            ])
        return copies

    def arrive(copies):
        copies[0].wait()
        for copy in copies[1:]:
            copy.wait_recv()

    def spread(h, w, places):
        return {j: remote(cache.at[0, h, w], cache.at[j, h, w], to_z(k)) for j, k in places}

    EDGE, NEXT = ((3, -2), (4, 2)), ((1, -1), (2, 1))

    parts0 = exchange(0)

    def pack(d, first, last, dst):
        for rr in range(first, last):
            dst[rr - first] = q[idx[d * RING + rr]]

    pack(0, 5, 8, relay_q.at[0])
    for d in range(1, PLANE):
        pack(d, 5, 8, fs.at[d])
    far_y = [remote(fs.at[d], relay_q.at[d], to_lane(d)) for d in range(1, PLANE)]
    pack(0, 0, 5, nq.at[0])
    for d in range(1, PLANE):
        pack(d, 0, 5, qs.at[d])
    near_y = [remote(qs.at[d], nq.at[d], to_lane(d)) for d in range(1, PLANE)]

    spread0 = []
    for w in range(2):
        arrive(parts0[w])
        spread0.append({**spread(0, w, EDGE), **spread(0, w, NEXT)})
    parts1 = exchange(1)

    block = HD // LEN
    rows = block * HD
    r_at = lax.broadcasted_iota(jnp.int32, (rows, HD), 0)
    c_at = lax.broadcasted_iota(jnp.int32, (rows, HD), 1)
    allowed = (r_at // HD == c_at // LEN) & (r_at % LEN >= c_at % LEN)

    def own_block(b, carry):
        keys, values = ck[b], cv[b]
        for h in range(HEADS):
            pieces = []
            for c in range(block):
                pieces += rows_of(q[b * block + c, :, h * SLOT : (h + 1) * SLOT])
            part = slice(h * HD, (h + 1) * HD)
            s = lax.dot_general(
                jnp.concatenate(pieces, axis=0), keys[:, part], (((1,), (1,)), ((), ())),
                preferred_element_type=jnp.float32,
            ) * SCALE
            s = jnp.where(allowed, s, -1e30)
            top = jnp.max(s, axis=1, keepdims=True)
            w = jnp.exp(s - top)
            total = jnp.sum(w, axis=1, keepdims=True)
            mixed = jnp.dot(
                w.astype(jnp.bfloat16), values[:, part], preferred_element_type=jnp.float32
            ) / total
            lse = top + jnp.log(total)
            for c in range(block):
                for g in range(GROUP):
                    at = c * HD + g * LEN
                    own[b * block + c, :, h * SLOT + g * HD : h * SLOT + (g + 1) * HD] = (
                        mixed[at : at + LEN]
                    )
                own_lse[b * block + c, h] = by_group(lse[c * HD : (c + 1) * HD])
        return carry

    lax.fori_loop(0, comps // block, own_block, 0)

    for copy in far_y:
        copy.wait_recv()
    half = PLANE // 2
    far_q = [
        remote(relay_q.at[:, 0], fq.at[pl.ds(0, 8)], to_z(1)),
        remote(relay_q.at[:, 1], fq.at[pl.ds(12, 8)], to_z(-1)),
        remote(relay_q.at[pl.ds(0, half), 2], fq.at[pl.ds(8, half)], to_z(2)),
        remote(relay_q.at[pl.ds(half, half), 2], fq.at[pl.ds(20, half)], to_z(-2)),
    ]

    def attend(queries, j, h):
        pieces = []
        for slot in queries:
            pieces += rows_of(slot)
        s = lax.dot_general(
            jnp.concatenate(pieces, axis=0), cache[j, h, 0], (((1,), (1,)), ((), ())),
            preferred_element_type=jnp.float32,
        )
        top = jnp.max(s, axis=1, keepdims=True)
        w = jnp.exp2((s - top) * (SCALE * LOG2E))
        total = jnp.sum(w, axis=1, keepdims=True)
        mixed = jnp.dot(w.astype(jnp.bfloat16), cache[j, h, 1], preferred_element_type=jnp.float32)
        mixed = (mixed / total).astype(jnp.bfloat16)
        lse = top * SCALE + jnp.log(total)
        results = []
        for n in range(len(queries)):
            at = n * HD
            hi, mid, low = split3(by_group(lse[at : at + HD]))
            tail = jnp.concatenate(
                [hi[:, :GROUP], mid[:, :GROUP], low[:, :GROUP], hi[:, 3 * GROUP :]], axis=1
            )
            results.append(
                [mixed[at + g * LEN : at + (g + 1) * LEN] for g in range(GROUP)] + [tail]
            )
        return results

    def put(dst, i, pieces):
        for g, piece in enumerate(pieces):
            dst[i + (slice(None), slice(g * HD, (g + 1) * HD))] = piece

    def head(h):
        return slice(h * SLOT, (h + 1) * SLOT)

    def near(h, first, last):
        def step(n, carry):
            j, d = first + n // (PLANE // 2), 2 * (n % (PLANE // 2))
            two = attend([nq[d, j, :, head(h)], nq[d + 1, j, :, head(h)]], j, h)
            for k in range(2):
                put(no, (h, d + k, j), two[k])
            return carry

        lax.fori_loop(0, (last - first) * (PLANE // 2), step, 0)

    def far(h):
        def step(n, carry):
            two = attend([fq[2 * n, :, head(h)], fq[2 * n + 1, :, head(h)]], 3 + n // 6, h)
            for k in range(2):
                put(fo, (h, 2 * n + k), two[k])
            return carry

        lax.fori_loop(0, 12, step, 0)

    returned = []

    def give_near(h, first, last):
        span = pl.ds(first, last - first)
        for d in range(1, PLANE):
            returned.append(remote(no.at[h, d, span], ret.at[h, pl.ds(d * RING + first, last - first)], to_lane(-d)))
        ret[h, first:last] = no[h, 0, first:last]

    def give_far(h):
        return [
            remote(fo.at[h, pl.ds(0, 8)], relay_o.at[h, 0], to_z(-1)),
            remote(fo.at[h, pl.ds(12, 8)], relay_o.at[h, 1], to_z(1)),
            remote(fo.at[h, pl.ds(8, half)], relay_o.at[h, 2, pl.ds(0, half)], to_z(-2)),
            remote(fo.at[h, pl.ds(20, half)], relay_o.at[h, 2, pl.ds(half, half)], to_z(2)),
        ]

    def pass_far(h, copies):
        for rr in range(3):
            for copy in (copies[rr : rr + 1] if rr < 2 else copies[2:]):
                copy.wait_recv()
            for d in range(1, PLANE):
                returned.append(remote(relay_o.at[h, rr, d], ret.at[h, d * RING + 5 + rr], to_lane(-d)))
            ret[h, 5 + rr] = relay_o[h, rr, 0]

    for w in range(2):
        arrive(parts1[w])
    for copy in near_y:
        copy.wait_recv()
    near(0, 0, 1)
    near(1, 0, 1)

    for copies in spread0:
        for copy in copies.values():
            copy.wait_send()
    edge1 = [spread(1, w, EDGE) for w in range(2)]
    for copies in spread0:
        for copy in copies.values():
            copy.wait_recv()
    near(0, 1, 5)
    give_near(0, 0, 5)
    for copy in far_q:
        copy.wait_recv()
    far(0)
    back0 = give_far(0)
    next1 = [spread(1, w, NEXT) for w in range(2)]

    for copies in edge1:
        for copy in copies.values():
            copy.wait_recv()
    far(1)
    back1 = give_far(1)
    pass_far(0, back0)
    near(1, 3, 5)
    give_near(1, 3, 5)
    for copies in next1:
        for copy in copies.values():
            copy.wait_recv()
    near(1, 1, 3)
    give_near(1, 0, 3)
    pass_far(1, back1)
    for copy in returned:
        copy.wait_recv()

    def blend(c, carry):
        for h in range(HEADS):
            slot = ret[h, pos[c]]
            tail = slot[:, SLOT:].astype(jnp.float32)
            far_lse = tail[:, :GROUP] + tail[:, GROUP : 2 * GROUP] + tail[:, 2 * GROUP : 3 * GROUP]
            near_lse = own_lse[c, h][:, :GROUP]
            ceiling = jnp.maximum(far_lse, near_lse)
            a, b = jnp.exp(far_lse - ceiling), jnp.exp(near_lse - ceiling)
            inverse = 1.0 / (a + b)
            a, b = a * inverse, b * inverse
            for g in range(GROUP):
                part = slice(h * SLOT + g * HD, h * SLOT + (g + 1) * HD)
                out[c, :, part] = (
                    slot[:, g * HD : (g + 1) * HD].astype(jnp.float32) * a[:, g : g + 1]
                    + own[c, :, part] * b[:, g : g + 1]
                ).astype(jnp.bfloat16)
        return carry

    lax.fori_loop(0, comps, blend, 0)
    already = {id(copy) for copies in spread0 for copy in copies.values()}
    for copy in sent:
        if id(copy) not in already:
            copy.wait_send()


def body(queries, comp_keys, comp_values, prefix_keys, prefix_values, prompt_of):
    comps = prompt_of.shape[0]
    dp = lax.axis_index("dp")
    prompt = prompt_of[:, 0]
    distance = (prompt // PLANE - dp // PLANE) % RING
    offset = (prompt % PLANE - dp % PLANE) % PLANE
    place = jnp.zeros_like(distance)
    for n, r in enumerate(ORDER):
        place = jnp.where(distance == r, n, place)
    pos = offset * RING + place
    slots = jnp.arange(PLANE * RING)
    idx = jnp.sum(
        jnp.where(pos[None, :] == slots[:, None], jnp.arange(comps)[None, :], 0), axis=1
    ).astype(jnp.int32)
    keys = prefix_keys.shape[0] * lax.axis_size("mp")
    bf16 = jnp.bfloat16
    blocks = comp_keys.shape[0] // HD
    vmem, smem = pl.BlockSpec(memory_space=pltpu.VMEM), pl.BlockSpec(memory_space=pltpu.SMEM)
    hbm = pl.BlockSpec(memory_space=pl.ANY)
    copies = 160
    out = pl.pallas_call(
        kernel,
        out_shape=jax.ShapeDtypeStruct((comps, LEN, queries.shape[1]), bf16),
        in_specs=[smem, smem, vmem, vmem, vmem, hbm, hbm],
        out_specs=vmem,
        scratch_shapes=[
            pltpu.VMEM((5, HEADS, 2, keys, HD), bf16),
            pltpu.VMEM((PLANE, 5, LEN, HEADS * SLOT), bf16),
            pltpu.VMEM((PLANE, 3, LEN, HEADS * SLOT), bf16),
            pltpu.VMEM((PLANE, 5, LEN, HEADS * SLOT), bf16),
            pltpu.VMEM((PLANE, 3, LEN, HEADS * SLOT), bf16),
            pltpu.VMEM((24, LEN, HEADS * SLOT), bf16),
            pltpu.VMEM((HEADS, PLANE, 5, LEN, WIDE), bf16),
            pltpu.VMEM((HEADS, 24, LEN, WIDE), bf16),
            pltpu.VMEM((HEADS, 3, PLANE, LEN, WIDE), bf16),
            pltpu.VMEM((HEADS, PLANE * RING, LEN, WIDE), bf16),
            pltpu.VMEM((comps, LEN, HEADS * SLOT), jnp.float32),
            pltpu.VMEM((comps, HEADS, LEN, HD), jnp.float32),
            pltpu.SemaphoreType.DMA((copies,)),
            pltpu.SemaphoreType.DMA((copies,)),
            pltpu.SemaphoreType.DMA((4,)),
        ],
        compiler_params=pltpu.CompilerParams(
            collective_id=0, has_side_effects=True, vmem_limit_bytes=60 * 1024 * 1024
        ),
        name="attend_all",
    )(
        idx,
        pos,
        queries.reshape(comps, LEN, -1),
        comp_keys.reshape(blocks, HD, -1),
        comp_values.reshape(blocks, HD, -1),
        prefix_keys,
        prefix_values,
    )
    return out.reshape(queries.shape)


def solution(mesh):
    placed = (
        P("dp", "mp"),
        P("dp", "mp"),
        P("dp", "mp"),
        P(("dp", "mp"), None),
        P(("dp", "mp"), None),
        P("dp", None),
    )
    return jax.shard_map(body, mesh=mesh, in_specs=placed, out_specs=P("dp", "mp"), check_vma=False)
```

```python
import functools
import math

import jax
import jax.numpy as jnp
from jax import lax
from jax.experimental import pallas as pl
from jax.experimental.pallas import tpu as pltpu
from jax.sharding import PartitionSpec as P

MESH = pl.DeviceIdType.MESH
HD = 128
LEN = 16
GROUP = 8
HEADS = 2
PLANE = 8
RING = 8
SLOT = GROUP * HD
WIDE = SLOT + HD
SCALE = 1.0 / math.sqrt(HD)
LOG2E = math.log2(math.e)
ORDER = (0, 1, 7, 2, 6, 3, 5, 4)


def split3(x):
    hi = x.astype(jnp.bfloat16)
    rest = x - hi.astype(jnp.float32)
    mid = rest.astype(jnp.bfloat16)
    low = (rest - mid.astype(jnp.float32)).astype(jnp.bfloat16)
    return hi, mid, low


def by_group(column):
    lane = lax.broadcasted_iota(jnp.int32, (LEN, HD), 1)
    out = jnp.zeros((LEN, HD), jnp.float32)
    for g in range(GROUP):
        out = jnp.where(lane == g, column[g * LEN : (g + 1) * LEN], out)
    return out


def rows_of(slot):
    return [slot[:, g * HD : (g + 1) * HD] for g in range(GROUP)]


def kernel(
    table, q_in, ck_in, cv_in, pk, pv, out,
    q, ck, cv, cache, qs, fs, nq, relay_q, fq, no, fo, relay_o, ret0, ret1, own, own_lse,
    send_sem, recv_sem, local_sem, load_sem,
):
    dp, x = lax.axis_index("dp"), lax.axis_index("mp")
    z, lane = dp // PLANE, dp % PLANE
    xs = lax.axis_size("mp")
    share = pk.shape[0]
    comps = q.shape[0]
    loads = [
        pltpu.make_async_copy(src, dst, load_sem.at[n])
        for n, (src, dst) in enumerate(((q_in, q), (ck_in, ck), (cv_in, cv)))
    ]
    for load in loads:
        load.start()

    def to_x(e):
        return (dp, (x + e) % xs)

    def to_z(k):
        return (((z + k + RING) % RING) * PLANE + lane, x)

    def to_lane(d):
        return (z * PLANE + (lane + d + PLANE) % PLANE, x)

    barrier = pltpu.get_barrier_semaphore()
    friends = (
        [to_x(e) for e in range(1, xs)]
        + [to_z(k) for k in (1, -1, 2, -2)]
        + [to_lane(d) for d in range(1, PLANE)]
    )
    for friend in friends:
        pl.semaphore_signal(barrier, 1, device_id=friend, device_id_type=MESH)

    def pack(dst, at, d, rr):
        dst[at] = q[table[rr * PLANE + d]]

    loads[0].wait()
    for rr in range(3):
        for d in range(PLANE):
            pack(fs, (rr, d), d, 5 + rr)
    pl.semaphore_wait(barrier, len(friends))

    count = [0]
    sent = []

    def remote(src, dst, device):
        n = count[0]
        count[0] += 1
        copy = pltpu.make_async_remote_copy(
            src_ref=src, dst_ref=dst, send_sem=send_sem.at[n], recv_sem=recv_sem.at[n],
            device_id=device, device_id_type=MESH,
        )
        copy.start()
        sent.append(copy)
        return copy

    def columns(e, h):
        return pl.ds(pl.multiple_of(((x + e) % xs) * (HEADS * HD) + h * HD, HD), HD)

    def exchange(h):
        copies = []
        for w, whole in enumerate((pk, pv)):
            mine = pltpu.make_async_copy(
                whole.at[:, columns(0, h)], cache.at[0, h, w, pl.ds(0, share)],
                local_sem.at[h * 2 + w],
            )
            mine.start()
            copies.append([mine] + [
                remote(whole.at[:, columns(e, h)], cache.at[0, h, w, pl.ds(e * share, share)], to_x(e))
                for e in range(1, xs)
            ])
        return copies

    def arrive(copies):
        copies[0].wait()
        for copy in copies[1:]:
            copy.wait_recv()

    def spread(h, w):
        return [remote(cache.at[0, h, w], cache.at[j, h, w], to_z(k)) for j, k in ((1, -1), (2, 1))]

    def relay(h, w, copies):
        for copy in copies:
            copy.wait_recv()
        return [remote(cache.at[j, h, w], cache.at[j + 2, h, w], to_z(k)) for j, k in ((1, -1), (2, 1))]

    half = PLANE // 2
    far_z = [
        remote(fs.at[0], relay_q.at[:, 0], to_z(1)),
        remote(fs.at[1], relay_q.at[:, 1], to_z(-1)),
        remote(fs.at[2, pl.ds(0, half)], relay_q.at[pl.ds(0, half), 2], to_z(2)),
        remote(fs.at[2, pl.ds(half, half)], relay_q.at[pl.ds(half, half), 2], to_z(-2)),
    ]
    parts0 = exchange(0)
    for rr in range(5):
        pack(nq, (0, rr), 0, rr)
        for d in range(1, PLANE):
            pack(qs, (d, rr), d, rr)
    near_y = [remote(qs.at[d], nq.at[d], to_lane(d)) for d in range(1, PLANE)]

    next0 = []
    for w in range(2):
        arrive(parts0[w])
        next0.append(spread(0, w))
    parts1 = exchange(1)

    block = HD // LEN
    rows = block * HD
    r_at = lax.broadcasted_iota(jnp.int32, (rows, HD), 0)
    c_at = lax.broadcasted_iota(jnp.int32, (rows, HD), 1)
    allowed = (r_at // HD == c_at // LEN) & (r_at % LEN >= c_at % LEN)

    def own_block(b, carry):
        keys, values = ck[b], cv[b]
        for h in range(HEADS):
            pieces = []
            for c in range(block):
                pieces += rows_of(q[b * block + c, :, h * SLOT : (h + 1) * SLOT])
            part = slice(h * HD, (h + 1) * HD)
            s = lax.dot_general(
                jnp.concatenate(pieces, axis=0), keys[:, part], (((1,), (1,)), ((), ())),
                preferred_element_type=jnp.float32,
            ) * SCALE
            s = jnp.where(allowed, s, -1e30)
            top = jnp.max(s, axis=1, keepdims=True)
            w = jnp.exp(s - top)
            total = jnp.sum(w, axis=1, keepdims=True)
            mixed = jnp.dot(
                w.astype(jnp.bfloat16), values[:, part], preferred_element_type=jnp.float32
            ) / total
            lse = top + jnp.log(total)
            for c in range(block):
                for g in range(GROUP):
                    at = c * HD + g * LEN
                    own[b * block + c, :, h * SLOT + g * HD : h * SLOT + (g + 1) * HD] = (
                        mixed[at : at + LEN]
                    )
                own_lse[b * block + c, h] = by_group(lse[c * HD : (c + 1) * HD])
        return carry

    for load in loads[1:]:
        load.wait()
    lax.fori_loop(0, comps // block, own_block, 0)

    next1 = []
    for w in range(2):
        arrive(parts1[w])
        next1.append(spread(1, w))
    for copy in far_z:
        copy.wait_recv()
    far_y = [remote(relay_q.at[d], fq.at[d], to_lane(d)) for d in range(1, PLANE)]
    fq[0] = relay_q[0]

    def attend(queries, j, h):
        pieces = []
        for slot in queries:
            pieces += rows_of(slot)
        s = lax.dot_general(
            jnp.concatenate(pieces, axis=0), cache[j, h, 0], (((1,), (1,)), ((), ())),
            preferred_element_type=jnp.float32,
        )
        top = jnp.max(s, axis=1, keepdims=True)
        w = jnp.exp2((s - top) * (SCALE * LOG2E))
        total = jnp.sum(w, axis=1, keepdims=True)
        mixed = jnp.dot(w.astype(jnp.bfloat16), cache[j, h, 1], preferred_element_type=jnp.float32)
        mixed = (mixed / total).astype(jnp.bfloat16)
        lse = top * SCALE + jnp.log(total)
        results = []
        for n in range(len(queries)):
            at = n * HD
            hi, mid, low = split3(by_group(lse[at : at + HD]))
            tail = jnp.concatenate(
                [hi[:, :GROUP], mid[:, :GROUP], low[:, :GROUP], hi[:, 3 * GROUP :]], axis=1
            )
            results.append(
                [mixed[at + g * LEN : at + (g + 1) * LEN] for g in range(GROUP)] + [tail]
            )
        return results

    def put(dst, i, pieces):
        for g, piece in enumerate(pieces):
            dst[i + (slice(None), slice(g * HD, (g + 1) * HD))] = piece

    ret = (ret0, ret1)

    def head(h):
        return slice(h * SLOT, (h + 1) * SLOT)

    def near(h, first, last):
        def step(n, carry):
            j, d = first + n // (PLANE // 2), 2 * (n % (PLANE // 2))
            two = attend([nq[d, j, :, head(h)], nq[d + 1, j, :, head(h)]], j, h)
            for k in range(2):
                put(no, (h, d + k, j), two[k])
            return carry

        lax.fori_loop(0, (last - first) * (PLANE // 2), step, 0)

    def far(h, k):
        def step(n, carry):
            d = 2 * n
            j = 3 + n // (half // 2) if k == 2 else 3 + k
            two = attend([fq[d, k, :, head(h)], fq[d + 1, k, :, head(h)]], j, h)
            for i in range(2):
                put(fo, (h, k, d + i), two[i])
            return carry

        lax.fori_loop(0, half, step, 0)
        relay_o[h, k, 0] = fo[h, k, 0]
        return [remote(fo.at[h, k, d], relay_o.at[h, k, d], to_lane(-d)) for d in range(1, PLANE)]

    returned = []

    def pass_far(h, k, copies):
        for copy in copies:
            copy.wait_recv()
        if k < 2:
            returned.append(remote(relay_o.at[h, k], ret[h].at[5 + k], to_z(2 * k - 1)))
        else:
            for n in range(2):
                span = pl.ds(n * half, half)
                returned.append(remote(relay_o.at[h, 2, span], ret[h].at[7, span], to_z(4 * n - 2)))

    def give_near(h, first, last):
        span = pl.ds(first, last - first)
        for d in range(1, PLANE):
            returned.append(remote(no.at[h, d, span], ret[h].at[span, d], to_lane(-d)))
        for j in range(first, last):
            ret[h][j, 0] = no[h, 0, j]

    for copy in near_y:
        copy.wait_recv()
    near(0, 0, 1)
    edge0 = [relay(0, w, next0[w]) for w in range(2)]
    near(1, 0, 1)
    near(0, 1, 3)
    give_near(0, 0, 3)
    edge1 = [relay(1, w, next1[w]) for w in range(2)]
    near(1, 1, 3)
    give_near(1, 0, 3)
    for copy in far_y:
        copy.wait_recv()
    for copies in edge0:
        for copy in copies:
            copy.wait_recv()
    back = {k: far(0, k) for k in (2, 0, 1)}
    near(0, 3, 5)
    give_near(0, 3, 5)
    for k in (2, 0, 1):
        pass_far(0, k, back[k])
    first = len(returned)
    for copies in edge1:
        for copy in copies:
            copy.wait_recv()
    back = {2: far(1, 2), 0: far(1, 0)}
    pass_far(1, 2, back[2])
    back[1] = far(1, 1)
    pass_far(1, 0, back[0])
    near(1, 3, 4)
    give_near(1, 3, 4)
    pass_far(1, 1, back[1])
    near(1, 4, 5)
    give_near(1, 4, 5)

    def blend(h):
        def step(n, carry):
            for c in [n * 4 + i for i in range(4)]:
                slot = ret[h][table[PLANE * RING + c], table[PLANE * RING + comps + c]]
                tail = slot[:, SLOT:].astype(jnp.float32)
                far_lse = tail[:, :GROUP] + tail[:, GROUP : 2 * GROUP] + tail[:, 2 * GROUP : 3 * GROUP]
                near_lse = own_lse[c, h][:, :GROUP]
                ceiling = jnp.maximum(far_lse, near_lse)
                a, b = jnp.exp(far_lse - ceiling), jnp.exp(near_lse - ceiling)
                a = a / (a + b)
                for g in range(GROUP):
                    part = slice(h * SLOT + g * HD, h * SLOT + (g + 1) * HD)
                    mine = own[c, :, part]
                    theirs = slot[:, g * HD : (g + 1) * HD].astype(jnp.float32)
                    out[c, :, part] = (mine + (theirs - mine) * a[:, g : g + 1]).astype(jnp.bfloat16)
            return carry

        lax.fori_loop(0, comps // 4, step, 0)

    for copy in returned[:first]:
        copy.wait_recv()
    blend(0)
    for copy in returned[first:]:
        copy.wait_recv()
    blend(1)
    for copy in sent:
        copy.wait_send()


def body(queries, comp_keys, comp_values, prefix_keys, prefix_values, prompt_of):
    comps = prompt_of.shape[0]
    dp = lax.axis_index("dp")
    prompt = prompt_of[:, 0]
    distance = (prompt // PLANE - dp // PLANE) % RING
    offset = (prompt % PLANE - dp % PLANE) % PLANE
    place = jnp.zeros_like(distance)
    for n, r in enumerate(ORDER):
        place = jnp.where(distance == r, n, place)
    pos = place * PLANE + offset
    t, c = jnp.arange(PLANE * RING + 2 * comps)[:, None], jnp.arange(comps)[None, :]
    entry = jnp.where(
        t < PLANE * RING,
        jnp.where(pos[None, :] == t, c, 0),
        jnp.where(c == t - PLANE * RING, place[None, :], 0)
        + jnp.where(c == t - PLANE * RING - comps, offset[None, :], 0),
    )
    table = jnp.sum(entry, axis=1).astype(jnp.int32)
    keys = prefix_keys.shape[0] * lax.axis_size("mp")
    bf16 = jnp.bfloat16
    blocks = comp_keys.shape[0] // HD
    vmem, smem = pl.BlockSpec(memory_space=pltpu.VMEM), pl.BlockSpec(memory_space=pltpu.SMEM)
    hbm = pl.BlockSpec(memory_space=pl.ANY)
    copies = 160
    out = pl.pallas_call(
        kernel,
        out_shape=jax.ShapeDtypeStruct((comps, LEN, queries.shape[1]), bf16),
        in_specs=[smem, hbm, hbm, hbm, hbm, hbm],
        out_specs=vmem,
        scratch_shapes=[
            pltpu.VMEM((comps, LEN, HEADS * SLOT), bf16),
            pltpu.VMEM((blocks, HD, HEADS * HD), bf16),
            pltpu.VMEM((blocks, HD, HEADS * HD), bf16),
            pltpu.VMEM((5, HEADS, 2, keys, HD), bf16),
            pltpu.VMEM((PLANE, 5, LEN, HEADS * SLOT), bf16),
            pltpu.VMEM((3, PLANE, LEN, HEADS * SLOT), bf16),
            pltpu.VMEM((PLANE, 5, LEN, HEADS * SLOT), bf16),
            pltpu.VMEM((PLANE, 3, LEN, HEADS * SLOT), bf16),
            pltpu.VMEM((PLANE, 3, LEN, HEADS * SLOT), bf16),
            pltpu.VMEM((HEADS, PLANE, 5, LEN, WIDE), bf16),
            pltpu.VMEM((HEADS, 3, PLANE, LEN, WIDE), bf16),
            pltpu.VMEM((HEADS, 3, PLANE, LEN, WIDE), bf16),
            pltpu.VMEM((RING, PLANE, LEN, WIDE), bf16),
            pltpu.VMEM((RING, PLANE, LEN, WIDE), bf16),
            pltpu.VMEM((comps, LEN, HEADS * SLOT), jnp.float32),
            pltpu.VMEM((comps, HEADS, LEN, HD), jnp.float32),
            pltpu.SemaphoreType.DMA((copies,)),
            pltpu.SemaphoreType.DMA((copies,)),
            pltpu.SemaphoreType.DMA((4,)),
            pltpu.SemaphoreType.DMA((3,)),
        ],
        compiler_params=pltpu.CompilerParams(
            collective_id=0, has_side_effects=True, vmem_limit_bytes=60 * 1024 * 1024
        ),
        name="attend_all",
    )(
        table,
        queries.reshape(comps, LEN, -1),
        comp_keys.reshape(blocks, HD, -1),
        comp_values.reshape(blocks, HD, -1),
        prefix_keys,
        prefix_values,
    )
    return out.reshape(queries.shape)


def solution(mesh):
    placed = (
        P("dp", "mp"),
        P("dp", "mp"),
        P("dp", "mp"),
        P(("dp", "mp"), None),
        P(("dp", "mp"), None),
        P("dp", None),
    )
    return jax.shard_map(body, mesh=mesh, in_specs=placed, out_specs=P("dp", "mp"), check_vma=False)
```

```python
import functools
import math

import jax
import jax.numpy as jnp
from jax import lax
from jax.experimental import pallas as pl
from jax.experimental.pallas import tpu as pltpu
from jax.sharding import PartitionSpec as P

MESH = pl.DeviceIdType.MESH
HD = 128
LEN = 16
GROUP = 8
HEADS = 2
PLANE = 8
RING = 8
SLOT = GROUP * HD
WIDE = SLOT + HD
SCALE = 1.0 / math.sqrt(HD)
LOG2E = math.log2(math.e)
ORDER = (0, 1, 7, 2, 6, 3, 5, 4)


def split3(x):
    hi = x.astype(jnp.bfloat16)
    rest = x - hi.astype(jnp.float32)
    mid = rest.astype(jnp.bfloat16)
    low = (rest - mid.astype(jnp.float32)).astype(jnp.bfloat16)
    return hi, mid, low


def by_group(column):
    lane = lax.broadcasted_iota(jnp.int32, (LEN, HD), 1)
    out = jnp.zeros((LEN, HD), jnp.float32)
    for g in range(GROUP):
        out = jnp.where(lane == g, column[g * LEN : (g + 1) * LEN], out)
    return out


def rows_of(slot):
    return [slot[:, g * HD : (g + 1) * HD] for g in range(GROUP)]


def kernel(
    table, prompt, q_in, ck_in, cv_in, pk, pv, out,
    q, ck, cv, cache, qs, fs, nq, relay_q, fq, no, fo, relay_o, ret0, ret1, own, own_lse,
    mixed, send_sem, recv_sem, local_sem, load_sem, out_sem,
):
    dp, x = lax.axis_index("dp"), lax.axis_index("mp")
    z, lane = dp // PLANE, dp % PLANE
    xs = lax.axis_size("mp")
    share = pk.shape[0]
    comps = q.shape[0]
    loads = [
        pltpu.make_async_copy(src, dst, load_sem.at[n])
        for n, (src, dst) in enumerate(((q_in, q), (ck_in, ck), (cv_in, cv)))
    ]
    for load in loads:
        load.start()

    def to_x(e):
        return (dp, (x + e) % xs)

    def to_z(k):
        return (((z + k + RING) % RING) * PLANE + lane, x)

    def to_lane(d):
        return (z * PLANE + (lane + d + PLANE) % PLANE, x)

    barrier = pltpu.get_barrier_semaphore()
    friends = (
        [to_x(e) for e in range(1, xs)]
        + [to_z(k) for k in (1, -1, 2, -2)]
        + [to_lane(d) for d in range(1, PLANE)]
    )
    for friend in friends:
        pl.semaphore_signal(barrier, 1, device_id=friend, device_id_type=MESH)

    def pack(dst, at, d, rr):
        dst[at] = q[table[rr * PLANE + d]]

    loads[0].wait()
    for rr in range(3):
        for d in range(PLANE):
            pack(fs, (rr, d), d, 5 + rr)
    pl.semaphore_wait(barrier, len(friends))

    count = [0]
    sent = []

    def remote(parts, src, dst):
        n = count[0]
        count[0] += 1
        for part_src, part_dst, device in parts:
            pltpu.make_async_remote_copy(
                src_ref=part_src, dst_ref=part_dst, send_sem=send_sem.at[n], recv_sem=recv_sem.at[n],
                device_id=device, device_id_type=MESH,
            ).start()
        whole = pltpu.make_async_remote_copy(
            src_ref=src, dst_ref=dst, send_sem=send_sem.at[n], recv_sem=recv_sem.at[n],
            device_id=parts[0][2], device_id_type=MESH,
        )
        sent.append(whole)
        return whole

    def columns(e, h):
        return pl.ds(pl.multiple_of(((x + e) % xs) * (HEADS * HD) + h * HD, HD), HD)

    def exchange(h):
        copies = []
        for w, whole in enumerate((pk, pv)):
            mine = pltpu.make_async_copy(
                whole.at[:, columns(0, h)], cache.at[0, h, w, pl.ds(0, share)],
                local_sem.at[h * 2 + w],
            )
            mine.start()
            others = cache.at[0, h, w, pl.ds(share, (xs - 1) * share)]
            copies.append((mine, remote(
                [
                    (whole.at[:, columns(e, h)], cache.at[0, h, w, pl.ds(e * share, share)], to_x(e))
                    for e in range(1, xs)
                ],
                others,
                others,
            )))
        return copies

    def arrive(copies):
        copies[0].wait()
        copies[1].wait_recv()

    def spread(h, w):
        both = cache.at[pl.ds(1, 2), h, w]
        return remote(
            [(cache.at[0, h, w], cache.at[j, h, w], to_z(k)) for j, k in ((1, -1), (2, 1))], both, both
        )

    def relay(h, w, copy):
        copy.wait_recv()
        return remote(
            [(cache.at[j, h, w], cache.at[j + 2, h, w], to_z(k)) for j, k in ((1, -1), (2, 1))],
            cache.at[pl.ds(1, 2), h, w],
            cache.at[pl.ds(3, 2), h, w],
        )

    half = PLANE // 2
    def along(k, src, dst, sign):
        if k < 2:
            return remote([(src, dst, to_z(sign * (1 - 2 * k)))], src, dst)
        spans = [pl.ds(n * half, half) for n in range(2)]
        return remote(
            [(src.at[span], dst.at[span], to_z(sign * (2 - 4 * n))) for n, span in enumerate(spans)], src, dst
        )

    far_z = [along(k, fs.at[k], relay_q.at[:, k], 1) for k in range(3)]
    parts0 = exchange(0)
    for rr in range(5):
        pack(nq, (0, rr), 0, rr)
        for d in range(1, PLANE):
            pack(qs, (d, rr), d, rr)
    lanes = pl.ds(1, PLANE - 1)
    near_y = remote(
        [(qs.at[d], nq.at[d], to_lane(d)) for d in range(1, PLANE)], qs.at[lanes], nq.at[lanes]
    )

    next0 = []
    for w in range(2):
        arrive(parts0[w])
        next0.append(spread(0, w))
    parts1 = exchange(1)

    block = HD // LEN
    rows = block * HD
    r_at = lax.broadcasted_iota(jnp.int32, (rows, HD), 0)
    c_at = lax.broadcasted_iota(jnp.int32, (rows, HD), 1)
    allowed = (r_at // HD == c_at // LEN) & (r_at % LEN >= c_at % LEN)

    def own_block(b, carry):
        keys, values = ck[b], cv[b]
        for h in range(HEADS):
            pieces = []
            for c in range(block):
                pieces += rows_of(q[b * block + c, :, h * SLOT : (h + 1) * SLOT])
            part = slice(h * HD, (h + 1) * HD)
            s = lax.dot_general(
                jnp.concatenate(pieces, axis=0), keys[:, part], (((1,), (1,)), ((), ())),
                preferred_element_type=jnp.float32,
            ) * SCALE
            s = jnp.where(allowed, s, -1e30)
            top = jnp.max(s, axis=1, keepdims=True)
            w = jnp.exp(s - top)
            total = jnp.sum(w, axis=1, keepdims=True)
            mixed = jnp.dot(
                w.astype(jnp.bfloat16), values[:, part], preferred_element_type=jnp.float32
            ) / total
            lse = top + jnp.log(total)
            for c in range(block):
                for g in range(GROUP):
                    at = c * HD + g * LEN
                    own[b * block + c, :, h * SLOT + g * HD : h * SLOT + (g + 1) * HD] = (
                        mixed[at : at + LEN]
                    )
                own_lse[b * block + c, h] = by_group(lse[c * HD : (c + 1) * HD])
        return carry

    for load in loads[1:]:
        load.wait()
    lax.fori_loop(0, comps // block, own_block, 0)

    next1 = []
    for w in range(2):
        arrive(parts1[w])
        next1.append(spread(1, w))
    for copy in far_z:
        copy.wait_recv()
    far_y = remote(
        [(relay_q.at[d], fq.at[d], to_lane(d)) for d in range(1, PLANE)], relay_q.at[lanes], fq.at[lanes]
    )
    fq[0] = relay_q[0]

    def attend(queries, j, h):
        scores, results = [], []
        for slot in queries:
            scores.append(lax.dot_general(
                jnp.concatenate(rows_of(slot[0]) + rows_of(slot[1]), axis=0), cache[j, h, 0],
                (((1,), (1,)), ((), ())), preferred_element_type=jnp.float32,
            ))
        for s in scores:
            top = jnp.max(s, axis=1, keepdims=True)
            w = jnp.exp2((s - top) * (SCALE * LOG2E))
            total = jnp.sum(w, axis=1, keepdims=True)
            mixed = jnp.dot(w.astype(jnp.bfloat16), cache[j, h, 1], preferred_element_type=jnp.float32)
            mixed = (mixed / total).astype(jnp.bfloat16)
            lse = top * SCALE + jnp.log(total)
            for at in (0, HD):
                hi, mid, low = split3(by_group(lse[at : at + HD]))
                tail = jnp.concatenate(
                    [hi[:, :GROUP], mid[:, :GROUP], low[:, :GROUP], hi[:, 3 * GROUP :]], axis=1
                )
                results.append(
                    [mixed[at + g * LEN : at + (g + 1) * LEN] for g in range(GROUP)] + [tail]
                )
        return results

    def put(dst, i, pieces):
        for g, piece in enumerate(pieces):
            dst[i + (slice(None), slice(g * HD, (g + 1) * HD))] = piece

    ret = (ret0, ret1)

    def head(h):
        return slice(h * SLOT, (h + 1) * SLOT)

    def near(h, first, last):
        def step(n, carry):
            j, d = first + n // 2, half * (n % 2)
            four = attend([[nq[d + i + k, j, :, head(h)] for k in range(2)] for i in (0, 2)], j, h)
            for k in range(4):
                put(no, (h, d + k, j), four[k])
            return carry

        lax.fori_loop(0, (last - first) * 2, step, 0)

    def far(h, k):
        def step(n, carry):
            d = half * n
            j = 3 + n if k == 2 else 3 + k
            four = attend([[fq[d + i + m, k, :, head(h)] for m in range(2)] for i in (0, 2)], j, h)
            for i in range(4):
                put(fo, (h, k, d + i), four[i])
            return carry

        lax.fori_loop(0, 2, step, 0)
        relay_o[h, k, 0] = fo[h, k, 0]
        return remote(
            [(fo.at[h, k, d], relay_o.at[h, k, d], to_lane(-d)) for d in range(1, PLANE)],
            fo.at[h, k, lanes],
            relay_o.at[h, k, lanes],
        )

    returned = []

    def pass_far(h, k, copy):
        copy.wait_recv()
        returned.append(along(k, relay_o.at[h, k], ret[h].at[5 + k], -1))

    def give_near(h, first, last):
        span = pl.ds(first, last - first)
        returned.append(remote(
            [(no.at[h, d, span], ret[h].at[span, d], to_lane(-d)) for d in range(1, PLANE)],
            no.at[h, lanes, span],
            ret[h].at[span, lanes],
        ))
        for j in range(first, last):
            ret[h][j, 0] = no[h, 0, j]

    near_y.wait_recv()
    near(0, 0, 1)
    edge0 = [relay(0, w, next0[w]) for w in range(2)]
    near(1, 0, 1)
    near(0, 1, 3)
    give_near(0, 0, 3)
    edge1 = [relay(1, w, next1[w]) for w in range(2)]
    near(1, 1, 3)
    give_near(1, 0, 3)
    far_y.wait_recv()
    for copy in edge0:
        copy.wait_recv()
    back = {k: far(0, k) for k in (2, 0, 1)}
    near(0, 3, 5)
    give_near(0, 3, 5)
    for k in (2, 0, 1):
        pass_far(0, k, back[k])
    first = len(returned)
    for copy in edge1:
        copy.wait_recv()
    back = {2: far(1, 2), 0: far(1, 0)}
    pass_far(1, 2, back[2])
    back[1] = far(1, 1)
    pass_far(1, 0, back[0])
    near(1, 3, 4)
    give_near(1, 3, 4)
    pass_far(1, 1, back[1])
    near(1, 4, 5)
    give_near(1, 4, 5)

    def write(h, n):
        span = pl.ds(n * 4, 4)
        return pltpu.make_async_copy(
            mixed.at[h, span], out.at[span, :, pl.ds(h * SLOT, SLOT)], out_sem.at[h, n]
        )

    def blend(h):
        def step(n, carry):
            for i in range(4):
                c = n * 4 + i
                distance = (prompt[c] // PLANE - z + RING) % RING
                place = jnp.where(
                    distance < 3,
                    distance + distance // 2,
                    jnp.where(distance < 6, 5 + (distance - 3) * 2 - (distance - 3) // 2 * 3, 16 - 2 * distance),
                )
                slot = ret[h][place, (prompt[c] - lane + PLANE) % PLANE]
                tail = slot[:, SLOT:].astype(jnp.float32)
                far_lse = tail[:, :GROUP] + tail[:, GROUP : 2 * GROUP] + tail[:, 2 * GROUP : 3 * GROUP]
                near_lse = own_lse[c, h][:, :GROUP]
                ceiling = jnp.maximum(far_lse, near_lse)
                a, b = jnp.exp(far_lse - ceiling), jnp.exp(near_lse - ceiling)
                a = a / (a + b)
                for g in range(GROUP):
                    part = slice(g * HD, (g + 1) * HD)
                    mine = own[c, :, h * SLOT + g * HD : h * SLOT + (g + 1) * HD]
                    theirs = slot[:, part].astype(jnp.float32)
                    mixed[h, c, :, part] = (mine + (theirs - mine) * a[:, g : g + 1]).astype(jnp.bfloat16)
            write(h, n).start()
            return carry

        lax.fori_loop(0, comps // 4, step, 0)

    for copy in returned[:first]:
        copy.wait_recv()
    blend(0)
    for copy in returned[first:]:
        copy.wait_recv()
    blend(1)
    for copy in sent:
        copy.wait_send()
    for h in range(HEADS):
        for n in range(comps // 4):
            write(h, n).wait()


def hand_over(src, dst, held, sems):
    parts, rows = held.shape[:2]
    spans = [pl.ds(n * rows, rows) for n in range(parts)]
    ins = [pltpu.make_async_copy(src.at[span], held.at[n], sems.at[0, n]) for n, span in enumerate(spans)]
    outs = [pltpu.make_async_copy(held.at[n], dst.at[span], sems.at[1, n]) for n, span in enumerate(spans)]
    for copy in ins:
        copy.start()
    for n in range(parts):
        ins[n].wait()
        outs[n].start()
    for copy in outs:
        copy.wait()


def body(queries, comp_keys, comp_values, prefix_keys, prefix_values, prompt_of):
    comps = prompt_of.shape[0]
    dp = lax.axis_index("dp")
    prompt = prompt_of[:, 0]
    slot = jnp.arange(PLANE * RING)
    place = slot // PLANE
    distance = jnp.zeros_like(place)
    for n, r in enumerate(ORDER):
        distance = jnp.where(place == n, r, distance)
    wanted = (dp // PLANE + distance) % RING * PLANE + (dp + slot) % PLANE
    named = prompt[None, :] == wanted[:, None]
    table = jnp.sum(jnp.where(named, jnp.arange(comps)[None, :], 0), axis=1).astype(jnp.int32)
    keys = prefix_keys.shape[0] * lax.axis_size("mp")
    bf16 = jnp.bfloat16
    blocks = comp_keys.shape[0] // HD
    vmem, smem = pl.BlockSpec(memory_space=pltpu.VMEM), pl.BlockSpec(memory_space=pltpu.SMEM)
    hbm = pl.BlockSpec(memory_space=pl.ANY)
    copies = 34
    out = pl.pallas_call(
        kernel,
        out_shape=jax.ShapeDtypeStruct((comps, LEN, queries.shape[1]), bf16),
        in_specs=[smem, smem, hbm, hbm, hbm, hbm, hbm],
        out_specs=hbm,
        scratch_shapes=[
            pltpu.VMEM((comps, LEN, HEADS * SLOT), bf16),
            pltpu.VMEM((blocks, HD, HEADS * HD), bf16),
            pltpu.VMEM((blocks, HD, HEADS * HD), bf16),
            pltpu.VMEM((5, HEADS, 2, keys, HD), bf16),
            pltpu.VMEM((PLANE, 5, LEN, HEADS * SLOT), bf16),
            pltpu.VMEM((3, PLANE, LEN, HEADS * SLOT), bf16),
            pltpu.VMEM((PLANE, 5, LEN, HEADS * SLOT), bf16),
            pltpu.VMEM((PLANE, 3, LEN, HEADS * SLOT), bf16),
            pltpu.VMEM((PLANE, 3, LEN, HEADS * SLOT), bf16),
            pltpu.VMEM((HEADS, PLANE, 5, LEN, WIDE), bf16),
            pltpu.VMEM((HEADS, 3, PLANE, LEN, WIDE), bf16),
            pltpu.VMEM((HEADS, 3, PLANE, LEN, WIDE), bf16),
            pltpu.VMEM((RING, PLANE, LEN, WIDE), bf16),
            pltpu.VMEM((RING, PLANE, LEN, WIDE), bf16),
            pltpu.VMEM((comps, LEN, HEADS * SLOT), jnp.float32),
            pltpu.VMEM((comps, HEADS, LEN, HD), jnp.float32),
            pltpu.VMEM((HEADS, comps, LEN, SLOT), bf16),
            pltpu.SemaphoreType.DMA((copies,)),
            pltpu.SemaphoreType.DMA((copies,)),
            pltpu.SemaphoreType.DMA((4,)),
            pltpu.SemaphoreType.DMA((3,)),
            pltpu.SemaphoreType.DMA((HEADS, comps // 4)),
        ],
        compiler_params=pltpu.CompilerParams(
            collective_id=0, has_side_effects=True, vmem_limit_bytes=60 * 1024 * 1024
        ),
        name="attend_all",
    )(
        table,
        prompt,
        queries.reshape(comps, LEN, -1),
        comp_keys.reshape(blocks, HD, -1),
        comp_values.reshape(blocks, HD, -1),
        prefix_keys,
        prefix_values,
    )
    return pl.pallas_call(
        hand_over,
        out_shape=jax.ShapeDtypeStruct(queries.shape, bf16),
        in_specs=[hbm],
        out_specs=hbm,
        scratch_shapes=[
            pltpu.VMEM((8, queries.shape[0] // 8, queries.shape[1]), bf16),
            pltpu.SemaphoreType.DMA((2, 8)),
        ],
        name="hand_over",
    )(out.reshape(queries.shape))


def solution(mesh):
    placed = (
        P("dp", "mp"),
        P("dp", "mp"),
        P("dp", "mp"),
        P(("dp", "mp"), None),
        P(("dp", "mp"), None),
        P("dp", None),
    )
    return jax.shard_map(body, mesh=mesh, in_specs=placed, out_specs=P("dp", "mp"), check_vma=False)
```

```python
import functools
import math

import jax
import jax.numpy as jnp
from jax import lax
from jax.experimental import pallas as pl
from jax.experimental.pallas import tpu as pltpu
from jax.sharding import PartitionSpec as P

MESH = pl.DeviceIdType.MESH
HD = 128
LEN = 16
GROUP = 8
HEADS = 2
PLANE = 8
RING = 8
SLOT = GROUP * HD
WIDE = SLOT + HD
SCALE = 1.0 / math.sqrt(HD)
LOG2E = math.log2(math.e)
ORDER = (0, 1, 7, 2, 6, 3, 5, 4)


def split3(x):
    hi = x.astype(jnp.bfloat16)
    rest = x - hi.astype(jnp.float32)
    mid = rest.astype(jnp.bfloat16)
    low = (rest - mid.astype(jnp.float32)).astype(jnp.bfloat16)
    return hi, mid, low


def by_group(column):
    lane = lax.broadcasted_iota(jnp.int32, (LEN, HD), 1)
    out = jnp.zeros((LEN, HD), jnp.float32)
    for g in range(GROUP):
        out = jnp.where(lane == g, column[g * LEN : (g + 1) * LEN], out)
    return out


def rows_of(slot):
    return [slot[:, g * HD : (g + 1) * HD] for g in range(GROUP)]


def kernel(
    table, prompt, q_in, ck_in, cv_in, pk, pv, out,
    q, ck, cv, cache, qs, fs, nq, relay_q, fq, no, fo, relay_o, ret0, ret1, own, own_lse,
    mixed, lse_out, lse_in, send_sem, recv_sem, local_sem, load_sem, out_sem,
):
    dp, x = lax.axis_index("dp"), lax.axis_index("mp")
    z, lane = dp // PLANE, dp % PLANE
    xs = lax.axis_size("mp")
    share = pk.shape[0]
    comps = q.shape[0]
    loads = [
        pltpu.make_async_copy(src, dst, load_sem.at[n])
        for n, (src, dst) in enumerate(((q_in, q), (ck_in, ck), (cv_in, cv)))
    ]
    for load in loads:
        load.start()

    def to_x(e):
        return (dp, (x + e) % xs)

    def to_z(k):
        return (((z + k + RING) % RING) * PLANE + lane, x)

    def to_lane(d):
        return (z * PLANE + (lane + d + PLANE) % PLANE, x)

    barrier = pltpu.get_barrier_semaphore()
    friends = (
        [to_x(e) for e in range(1, xs)]
        + [to_z(k) for k in (1, -1, 2, -2)]
        + [to_lane(d) for d in range(1, PLANE)]
    )
    for friend in friends:
        pl.semaphore_signal(barrier, 1, device_id=friend, device_id_type=MESH)

    def pack(dst, at, d, rr):
        dst[at] = q[table[rr * PLANE + d]]

    loads[0].wait()
    for rr in range(3):
        for d in range(PLANE):
            pack(fs, (rr, d), d, 5 + rr)
    pl.semaphore_wait(barrier, len(friends))

    count = [0]
    sent = []

    def remote(parts, src, dst):
        n = count[0]
        count[0] += 1
        for part_src, part_dst, device in parts:
            pltpu.make_async_remote_copy(
                src_ref=part_src, dst_ref=part_dst, send_sem=send_sem.at[n], recv_sem=recv_sem.at[n],
                device_id=device, device_id_type=MESH,
            ).start()
        whole = pltpu.make_async_remote_copy(
            src_ref=src, dst_ref=dst, send_sem=send_sem.at[n], recv_sem=recv_sem.at[n],
            device_id=parts[0][2], device_id_type=MESH,
        )
        sent.append(whole)
        return whole

    def columns(e, h):
        return pl.ds(pl.multiple_of(((x + e) % xs) * (HEADS * HD) + h * HD, HD), HD)

    def exchange(h):
        copies = []
        for w, whole in enumerate((pk, pv)):
            mine = pltpu.make_async_copy(
                whole.at[:, columns(0, h)], cache.at[0, h, w, pl.ds(0, share)],
                local_sem.at[h * 2 + w],
            )
            mine.start()
            others = cache.at[0, h, w, pl.ds(share, (xs - 1) * share)]
            copies.append((mine, remote(
                [
                    (whole.at[:, columns(e, h)], cache.at[0, h, w, pl.ds(e * share, share)], to_x(e))
                    for e in range(1, xs)
                ],
                others,
                others,
            )))
        return copies

    def arrive(copies):
        copies[0].wait()
        copies[1].wait_recv()

    def spread(h, w):
        both = cache.at[pl.ds(1, 2), h, w]
        return remote(
            [(cache.at[0, h, w], cache.at[j, h, w], to_z(k)) for j, k in ((1, -1), (2, 1))], both, both
        )

    def relay(h, w, copy):
        copy.wait_recv()
        return remote(
            [(cache.at[j, h, w], cache.at[j + 2, h, w], to_z(k)) for j, k in ((1, -1), (2, 1))],
            cache.at[pl.ds(1, 2), h, w],
            cache.at[pl.ds(3, 2), h, w],
        )

    half = PLANE // 2
    def along(k, src, dst, sign):
        if k < 2:
            return remote([(src, dst, to_z(sign * (1 - 2 * k)))], src, dst)
        part = src.shape[0] // 2
        spans = [pl.ds(n * part, part) for n in range(2)]
        return remote(
            [(src.at[span], dst.at[span], to_z(sign * (2 - 4 * n))) for n, span in enumerate(spans)], src, dst
        )

    far_z = [along(k, fs.at[k], relay_q.at[:, k], 1) for k in range(3)]
    parts0 = exchange(0)
    for rr in range(5):
        pack(nq, (0, rr), 0, rr)
        for d in range(1, PLANE):
            pack(qs, (d, rr), d, rr)
    lanes = pl.ds(1, PLANE - 1)
    near_y = remote(
        [(qs.at[d], nq.at[d], to_lane(d)) for d in range(1, PLANE)], qs.at[lanes], nq.at[lanes]
    )

    next0 = []
    for w in range(2):
        arrive(parts0[w])
        next0.append(spread(0, w))
    parts1 = exchange(1)

    block = HD // LEN
    rows = block * HD
    r_at = lax.broadcasted_iota(jnp.int32, (rows, HD), 0)
    c_at = lax.broadcasted_iota(jnp.int32, (rows, HD), 1)
    allowed = (r_at // HD == c_at // LEN) & (r_at % LEN >= c_at % LEN)

    def own_block(b, carry):
        keys, values = ck[b], cv[b]
        for h in range(HEADS):
            pieces = []
            for c in range(block):
                pieces += rows_of(q[b * block + c, :, h * SLOT : (h + 1) * SLOT])
            part = slice(h * HD, (h + 1) * HD)
            s = lax.dot_general(
                jnp.concatenate(pieces, axis=0), keys[:, part], (((1,), (1,)), ((), ())),
                preferred_element_type=jnp.float32,
            ) * SCALE
            s = jnp.where(allowed, s, -1e30)
            top = jnp.max(s, axis=1, keepdims=True)
            w = jnp.exp(s - top)
            total = jnp.sum(w, axis=1, keepdims=True)
            mixed = jnp.dot(
                w.astype(jnp.bfloat16), values[:, part], preferred_element_type=jnp.float32
            ) / total
            lse = top + jnp.log(total)
            for c in range(block):
                for g in range(GROUP):
                    at = c * HD + g * LEN
                    own[b * block + c, :, h * SLOT + g * HD : h * SLOT + (g + 1) * HD] = (
                        mixed[at : at + LEN]
                    )
                own_lse[b * block + c, h] = by_group(lse[c * HD : (c + 1) * HD])
        return carry

    for load in loads[1:]:
        load.wait()
    lax.fori_loop(0, comps // block, own_block, 0)

    next1 = []
    for w in range(2):
        arrive(parts1[w])
        next1.append(spread(1, w))
    for copy in far_z:
        copy.wait_recv()
    far_y = remote(
        [(relay_q.at[d], fq.at[d], to_lane(d)) for d in range(1, PLANE)], relay_q.at[lanes], fq.at[lanes]
    )
    fq[0] = relay_q[0]

    def attend(queries, j, h):
        scores, results = [], []
        for slot in queries:
            scores.append(lax.dot_general(
                jnp.concatenate(rows_of(slot[0]) + rows_of(slot[1]), axis=0), cache[j, h, 0],
                (((1,), (1,)), ((), ())), preferred_element_type=jnp.float32,
            ))
        for s in scores:
            top = jnp.max(s, axis=1, keepdims=True)
            w = jnp.exp2((s - top) * (SCALE * LOG2E))
            total = jnp.sum(w, axis=1, keepdims=True)
            mixed = jnp.dot(w.astype(jnp.bfloat16), cache[j, h, 1], preferred_element_type=jnp.float32)
            mixed = (mixed / total).astype(jnp.bfloat16)
            lse = top * SCALE + jnp.log(total)
            for at in (0, HD):
                hi, mid, low = split3(by_group(lse[at : at + HD]))
                tail = jnp.concatenate(
                    [hi[:, :GROUP], mid[:, :GROUP], low[:, :GROUP], hi[:, 3 * GROUP :]], axis=1
                )
                results.append(
                    [mixed[at + g * LEN : at + (g + 1) * LEN] for g in range(GROUP)] + [tail]
                )
        return results

    def put(dst, i, pieces):
        for g, piece in enumerate(pieces):
            dst[i + (slice(None), slice(g * HD, (g + 1) * HD))] = piece

    ret = (ret0, ret1)

    def head(h):
        return slice(h * SLOT, (h + 1) * SLOT)

    def near(h, first, last):
        def step(n, carry):
            j, d = first + n // 2, half * (n % 2)
            four = attend([[nq[d + i + k, j, :, head(h)] for k in range(2)] for i in (0, 2)], j, h)
            for k in range(4):
                put(no, (h, d + k, j), four[k])
            return carry

        lax.fori_loop(0, (last - first) * 2, step, 0)

    def far(h, k):
        def step(n, carry):
            d = half * n
            j = 3 + n if k == 2 else 3 + k
            four = attend([[fq[d + i + m, k, :, head(h)] for m in range(2)] for i in (0, 2)], j, h)
            for i in range(4):
                put(fo, (h, k, d + i), four[i])
            return carry

        lax.fori_loop(0, 2, step, 0)
        relay_o[h, k, 0] = fo[h, k, 0]
        return remote(
            [(fo.at[h, k, d], relay_o.at[h, k, d], to_lane(-d)) for d in range(1, PLANE)],
            fo.at[h, k, lanes],
            relay_o.at[h, k, lanes],
        )

    returned = []

    def pass_far(h, k, copy):
        copy.wait_recv()
        columns = pl.ds(0, SLOT)
        returned.append(along(k, relay_o.at[h, k, :, :, columns], ret[h].at[5 + k, :, :, columns], -1))
        lanes_at = lax.broadcasted_iota(jnp.int32, (LEN, HD), 1)
        for n in range(2):
            tile = jnp.zeros((LEN, HD), jnp.float32)
            for i in range(half):
                tail = relay_o[h, k, n * half + i, :, SLOT:].astype(jnp.float32)
                tail = jnp.where(lanes_at < 3 * GROUP, tail, 0.0)
                tile += pltpu.roll(tail, 3 * GROUP * i, 1) if i else tail
            lse_out[h, k, n] = tile.astype(jnp.bfloat16)
        returned.append(along(k, lse_out.at[h, k], lse_in.at[h, k], -1))

    def unpack(h):
        for k in range(3):
            for n in range(2):
                tile = lse_in[h, k, n].astype(jnp.float32)
                for i in range(half):
                    tail = pltpu.roll(tile, HD - 3 * GROUP * i, 1) if i else tile
                    ret[h][5 + k, n * half + i, :, SLOT:] = tail.astype(jnp.bfloat16)

    def give_near(h, first, last):
        span = pl.ds(first, last - first)
        returned.append(remote(
            [(no.at[h, d, span], ret[h].at[span, d], to_lane(-d)) for d in range(1, PLANE)],
            no.at[h, lanes, span],
            ret[h].at[span, lanes],
        ))
        for j in range(first, last):
            ret[h][j, 0] = no[h, 0, j]

    near_y.wait_recv()
    near(0, 0, 1)
    edge0 = [relay(0, w, next0[w]) for w in range(2)]
    near(1, 0, 1)
    near(0, 1, 3)
    give_near(0, 0, 3)
    edge1 = [relay(1, w, next1[w]) for w in range(2)]
    near(1, 1, 3)
    give_near(1, 0, 3)
    far_y.wait_recv()
    for copy in edge0:
        copy.wait_recv()
    back = {k: far(0, k) for k in (2, 0, 1)}
    near(0, 3, 5)
    give_near(0, 3, 5)
    for copy in edge1:
        copy.wait_recv()
    for k in (2, 0, 1):
        pass_far(0, k, back[k])
    first = len(returned)
    back = {2: far(1, 2), 0: far(1, 0)}
    pass_far(1, 2, back[2])
    back[1] = far(1, 1)
    pass_far(1, 0, back[0])
    near(1, 3, 4)
    give_near(1, 3, 4)
    pass_far(1, 1, back[1])
    near(1, 4, 5)
    give_near(1, 4, 5)

    def write(h, n):
        span = pl.ds(n * 4, 4)
        return pltpu.make_async_copy(
            mixed.at[h, span], out.at[span, :, pl.ds(h * SLOT, SLOT)], out_sem.at[h, n]
        )

    def blend(h):
        def step(n, carry):
            for i in range(4):
                c = n * 4 + i
                distance = (prompt[c] // PLANE - z + RING) % RING
                place = jnp.where(
                    distance < 3,
                    distance + distance // 2,
                    jnp.where(distance < 6, 5 + (distance - 3) * 2 - (distance - 3) // 2 * 3, 16 - 2 * distance),
                )
                slot = ret[h][place, (prompt[c] - lane + PLANE) % PLANE]
                tail = slot[:, SLOT:].astype(jnp.float32)
                far_lse = tail[:, :GROUP] + tail[:, GROUP : 2 * GROUP] + tail[:, 2 * GROUP : 3 * GROUP]
                near_lse = own_lse[c, h][:, :GROUP]
                ceiling = jnp.maximum(far_lse, near_lse)
                a, b = jnp.exp(far_lse - ceiling), jnp.exp(near_lse - ceiling)
                a = a / (a + b)
                for g in range(GROUP):
                    part = slice(g * HD, (g + 1) * HD)
                    mine = own[c, :, h * SLOT + g * HD : h * SLOT + (g + 1) * HD]
                    theirs = slot[:, part].astype(jnp.float32)
                    mixed[h, c, :, part] = (mine + (theirs - mine) * a[:, g : g + 1]).astype(jnp.bfloat16)
            write(h, n).start()
            return carry

        lax.fori_loop(0, comps // 4, step, 0)

    for copy in returned[:first]:
        copy.wait_recv()
    unpack(0)
    blend(0)
    for copy in returned[first:]:
        copy.wait_recv()
    unpack(1)
    blend(1)
    for copy in sent:
        copy.wait_send()
    for h in range(HEADS):
        for n in range(comps // 4):
            write(h, n).wait()


def hand_over(src, dst, held, sems):
    parts, rows = held.shape[:2]
    spans = [pl.ds(n * rows, rows) for n in range(parts)]
    ins = [pltpu.make_async_copy(src.at[span], held.at[n], sems.at[0, n]) for n, span in enumerate(spans)]
    outs = [pltpu.make_async_copy(held.at[n], dst.at[span], sems.at[1, n]) for n, span in enumerate(spans)]
    for copy in ins:
        copy.start()
    for n in range(parts):
        ins[n].wait()
        outs[n].start()
    for copy in outs:
        copy.wait()


def body(queries, comp_keys, comp_values, prefix_keys, prefix_values, prompt_of):
    comps = prompt_of.shape[0]
    dp = lax.axis_index("dp")
    prompt = prompt_of[:, 0]
    slot = jnp.arange(PLANE * RING)
    place = slot // PLANE
    distance = jnp.zeros_like(place)
    for n, r in enumerate(ORDER):
        distance = jnp.where(place == n, r, distance)
    wanted = (dp // PLANE + distance) % RING * PLANE + (dp + slot) % PLANE
    named = prompt[None, :] == wanted[:, None]
    table = jnp.sum(jnp.where(named, jnp.arange(comps)[None, :], 0), axis=1).astype(jnp.int32)
    keys = prefix_keys.shape[0] * lax.axis_size("mp")
    bf16 = jnp.bfloat16
    blocks = comp_keys.shape[0] // HD
    vmem, smem = pl.BlockSpec(memory_space=pltpu.VMEM), pl.BlockSpec(memory_space=pltpu.SMEM)
    hbm = pl.BlockSpec(memory_space=pl.ANY)
    copies = 40
    out = pl.pallas_call(
        kernel,
        out_shape=jax.ShapeDtypeStruct((comps, LEN, queries.shape[1]), bf16),
        in_specs=[smem, smem, hbm, hbm, hbm, hbm, hbm],
        out_specs=hbm,
        scratch_shapes=[
            pltpu.VMEM((comps, LEN, HEADS * SLOT), bf16),
            pltpu.VMEM((blocks, HD, HEADS * HD), bf16),
            pltpu.VMEM((blocks, HD, HEADS * HD), bf16),
            pltpu.VMEM((5, HEADS, 2, keys, HD), bf16),
            pltpu.VMEM((PLANE, 5, LEN, HEADS * SLOT), bf16),
            pltpu.VMEM((3, PLANE, LEN, HEADS * SLOT), bf16),
            pltpu.VMEM((PLANE, 5, LEN, HEADS * SLOT), bf16),
            pltpu.VMEM((PLANE, 3, LEN, HEADS * SLOT), bf16),
            pltpu.VMEM((PLANE, 3, LEN, HEADS * SLOT), bf16),
            pltpu.VMEM((HEADS, PLANE, 5, LEN, WIDE), bf16),
            pltpu.VMEM((HEADS, 3, PLANE, LEN, WIDE), bf16),
            pltpu.VMEM((HEADS, 3, PLANE, LEN, WIDE), bf16),
            pltpu.VMEM((RING, PLANE, LEN, WIDE), bf16),
            pltpu.VMEM((RING, PLANE, LEN, WIDE), bf16),
            pltpu.VMEM((comps, LEN, HEADS * SLOT), jnp.float32),
            pltpu.VMEM((comps, HEADS, LEN, HD), jnp.float32),
            pltpu.VMEM((HEADS, comps, LEN, SLOT), bf16),
            pltpu.VMEM((HEADS, 3, 2, LEN, HD), bf16),
            pltpu.VMEM((HEADS, 3, 2, LEN, HD), bf16),
            pltpu.SemaphoreType.DMA((copies,)),
            pltpu.SemaphoreType.DMA((copies,)),
            pltpu.SemaphoreType.DMA((4,)),
            pltpu.SemaphoreType.DMA((3,)),
            pltpu.SemaphoreType.DMA((HEADS, comps // 4)),
        ],
        compiler_params=pltpu.CompilerParams(
            collective_id=0, has_side_effects=True, vmem_limit_bytes=60 * 1024 * 1024
        ),
        name="attend_all",
    )(
        table,
        prompt,
        queries.reshape(comps, LEN, -1),
        comp_keys.reshape(blocks, HD, -1),
        comp_values.reshape(blocks, HD, -1),
        prefix_keys,
        prefix_values,
    )
    return pl.pallas_call(
        hand_over,
        out_shape=jax.ShapeDtypeStruct(queries.shape, bf16),
        in_specs=[hbm],
        out_specs=hbm,
        scratch_shapes=[
            pltpu.VMEM((8, queries.shape[0] // 8, queries.shape[1]), bf16),
            pltpu.SemaphoreType.DMA((2, 8)),
        ],
        name="hand_over",
    )(out.reshape(queries.shape))


def solution(mesh):
    placed = (
        P("dp", "mp"),
        P("dp", "mp"),
        P("dp", "mp"),
        P(("dp", "mp"), None),
        P(("dp", "mp"), None),
        P("dp", None),
    )
    return jax.shard_map(body, mesh=mesh, in_specs=placed, out_specs=P("dp", "mp"), check_vma=False)
```

```python
import functools
import math

import jax
import jax.numpy as jnp
from jax import lax
from jax.experimental import pallas as pl
from jax.experimental.pallas import tpu as pltpu
from jax.sharding import PartitionSpec as P

MESH = pl.DeviceIdType.MESH
HD = 128
LEN = 16
GROUP = 8
HEADS = 2
PLANE = 8
RING = 8
SLOT = GROUP * HD
WIDE = SLOT + HD
SCALE = 1.0 / math.sqrt(HD)
LOG2E = math.log2(math.e)
ORDER = (0, 1, 7, 2, 6, 3, 5, 4)


def split3(x):
    hi = x.astype(jnp.bfloat16)
    rest = x - hi.astype(jnp.float32)
    mid = rest.astype(jnp.bfloat16)
    low = (rest - mid.astype(jnp.float32)).astype(jnp.bfloat16)
    return hi, mid, low


def by_group(column):
    lane = lax.broadcasted_iota(jnp.int32, (LEN, HD), 1)
    out = jnp.zeros((LEN, HD), jnp.float32)
    for g in range(GROUP):
        out = jnp.where(lane == g, column[g * LEN : (g + 1) * LEN], out)
    return out


def rows_of(slot):
    return [slot[:, g * HD : (g + 1) * HD] for g in range(GROUP)]


def kernel(
    table, prompt, q_in, ck_in, cv_in, pk, pv, out,
    q, ck, cv, cache, qs, fs, nq, relay_q, fq, no, fo, relay_o, ret0, ret1, own, own_lse,
    mixed, lse_out, lse_in, send_sem, recv_sem, local_sem, load_sem, out_sem,
):
    dp, x = lax.axis_index("dp"), lax.axis_index("mp")
    z, lane = dp // PLANE, dp % PLANE
    xs = lax.axis_size("mp")
    share = pk.shape[0]
    comps = q.shape[0]
    loads = [
        pltpu.make_async_copy(src, dst, load_sem.at[n])
        for n, (src, dst) in enumerate(((q_in, q), (ck_in, ck), (cv_in, cv)))
    ]
    for load in loads:
        load.start()

    def to_x(e):
        return (dp, (x + e) % xs)

    def to_z(k):
        return (((z + k + RING) % RING) * PLANE + lane, x)

    def to_lane(d):
        return (z * PLANE + (lane + d + PLANE) % PLANE, x)

    barrier = pltpu.get_barrier_semaphore()
    friends = (
        [to_x(e) for e in range(1, xs)]
        + [to_z(k) for k in (1, -1, 2, -2)]
        + [to_lane(d) for d in range(1, PLANE)]
    )
    for friend in friends:
        pl.semaphore_signal(barrier, 1, device_id=friend, device_id_type=MESH)

    def pack(dst, at, d, rr):
        dst[at] = q[table[rr * PLANE + d]]

    loads[0].wait()
    for rr in range(3):
        for d in range(PLANE):
            pack(fs, (rr, d), d, 5 + rr)
    pl.semaphore_wait(barrier, len(friends))

    count = [0]
    sent = []

    def remote(parts, src, dst):
        n = count[0]
        count[0] += 1
        for part_src, part_dst, device in parts:
            pltpu.make_async_remote_copy(
                src_ref=part_src, dst_ref=part_dst, send_sem=send_sem.at[n], recv_sem=recv_sem.at[n],
                device_id=device, device_id_type=MESH,
            ).start()
        whole = pltpu.make_async_remote_copy(
            src_ref=src, dst_ref=dst, send_sem=send_sem.at[n], recv_sem=recv_sem.at[n],
            device_id=parts[0][2], device_id_type=MESH,
        )
        sent.append(whole)
        return whole

    def columns(e, h):
        return pl.ds(pl.multiple_of(((x + e) % xs) * (HEADS * HD) + h * HD, HD), HD)

    def exchange(h):
        copies = []
        for w, whole in enumerate((pk, pv)):
            mine = pltpu.make_async_copy(
                whole.at[:, columns(0, h)], cache.at[0, h, w, pl.ds(0, share)],
                local_sem.at[h * 2 + w],
            )
            mine.start()
            others = cache.at[0, h, w, pl.ds(share, (xs - 1) * share)]
            copies.append((mine, remote(
                [
                    (whole.at[:, columns(e, h)], cache.at[0, h, w, pl.ds(e * share, share)], to_x(e))
                    for e in range(1, xs)
                ],
                others,
                others,
            )))
        return copies

    def arrive(copies):
        copies[0].wait()
        copies[1].wait_recv()

    def spread(h, w):
        both = cache.at[pl.ds(1, 2), h, w]
        return remote(
            [(cache.at[0, h, w], cache.at[j, h, w], to_z(k)) for j, k in ((1, -1), (2, 1))], both, both
        )

    def relay(h, w, copy):
        copy.wait_recv()
        return remote(
            [(cache.at[j, h, w], cache.at[j + 2, h, w], to_z(k)) for j, k in ((1, -1), (2, 1))],
            cache.at[pl.ds(1, 2), h, w],
            cache.at[pl.ds(3, 2), h, w],
        )

    half = PLANE // 2
    def along(k, src, dst, sign):
        if k < 2:
            return remote([(src, dst, to_z(sign * (1 - 2 * k)))], src, dst)
        part = src.shape[0] // 2
        spans = [pl.ds(n * part, part) for n in range(2)]
        return remote(
            [(src.at[span], dst.at[span], to_z(sign * (2 - 4 * n))) for n, span in enumerate(spans)], src, dst
        )

    far_z = [along(k, fs.at[k], relay_q.at[:, k], 1) for k in range(3)]
    parts0 = exchange(0)
    for rr in range(5):
        pack(nq, (0, rr), 0, rr)
        for d in range(1, PLANE):
            pack(qs, (d, rr), d, rr)
    lanes = pl.ds(1, PLANE - 1)
    near_y = remote(
        [(qs.at[d], nq.at[d], to_lane(d)) for d in range(1, PLANE)], qs.at[lanes], nq.at[lanes]
    )

    next0 = []
    for w in range(2):
        arrive(parts0[w])
        next0.append(spread(0, w))
    parts1 = exchange(1)

    block = HD // LEN
    rows = block * HD
    r_at = lax.broadcasted_iota(jnp.int32, (rows, HD), 0)
    c_at = lax.broadcasted_iota(jnp.int32, (rows, HD), 1)
    allowed = (r_at // HD == c_at // LEN) & (r_at % LEN >= c_at % LEN)

    def own_block(b, carry):
        keys, values = ck[b], cv[b]
        for h in range(HEADS):
            pieces = []
            for c in range(block):
                pieces += rows_of(q[b * block + c, :, h * SLOT : (h + 1) * SLOT])
            part = slice(h * HD, (h + 1) * HD)
            s = lax.dot_general(
                jnp.concatenate(pieces, axis=0), keys[:, part], (((1,), (1,)), ((), ())),
                preferred_element_type=jnp.float32,
            ) * SCALE
            s = jnp.where(allowed, s, -1e30)
            top = jnp.max(s, axis=1, keepdims=True)
            w = jnp.exp(s - top)
            total = jnp.sum(w, axis=1, keepdims=True)
            mixed = jnp.dot(
                w.astype(jnp.bfloat16), values[:, part], preferred_element_type=jnp.float32
            ) / total
            lse = top + jnp.log(total)
            for c in range(block):
                for g in range(GROUP):
                    at = c * HD + g * LEN
                    own[b * block + c, :, h * SLOT + g * HD : h * SLOT + (g + 1) * HD] = (
                        mixed[at : at + LEN]
                    )
                own_lse[b * block + c, h] = by_group(lse[c * HD : (c + 1) * HD])
        return carry

    for load in loads[1:]:
        load.wait()
    lax.fori_loop(0, comps // block, own_block, 0)

    next1 = []
    for w in range(2):
        arrive(parts1[w])
        next1.append(spread(1, w))
    for copy in far_z:
        copy.wait_recv()
    far_y = remote(
        [(relay_q.at[d], fq.at[d], to_lane(d)) for d in range(1, PLANE)], relay_q.at[lanes], fq.at[lanes]
    )
    fq[0] = relay_q[0]

    def attend(queries, j, h):
        scores, results = [], []
        for slot in queries:
            scores.append(lax.dot_general(
                jnp.concatenate(rows_of(slot[0]) + rows_of(slot[1]), axis=0), cache[j, h, 0],
                (((1,), (1,)), ((), ())), preferred_element_type=jnp.float32,
            ))
        for s in scores:
            top = jnp.max(s, axis=1, keepdims=True)
            w = jnp.exp2((s - top) * (SCALE * LOG2E))
            total = jnp.sum(w, axis=1, keepdims=True)
            mixed = jnp.dot(w.astype(jnp.bfloat16), cache[j, h, 1], preferred_element_type=jnp.float32)
            mixed = (mixed / total).astype(jnp.bfloat16)
            lse = top * SCALE + jnp.log(total)
            for at in (0, HD):
                hi, mid, low = split3(by_group(lse[at : at + HD]))
                tail = jnp.concatenate(
                    [hi[:, :GROUP], mid[:, :GROUP], low[:, :GROUP], hi[:, 3 * GROUP :]], axis=1
                )
                results.append(
                    [mixed[at + g * LEN : at + (g + 1) * LEN] for g in range(GROUP)] + [tail]
                )
        return results

    def put(dst, i, pieces):
        for g, piece in enumerate(pieces):
            dst[i + (slice(None), slice(g * HD, (g + 1) * HD))] = piece

    ret = (ret0, ret1)

    def head(h):
        return slice(h * SLOT, (h + 1) * SLOT)

    def near(h, first, last):
        def step(n, carry):
            j, d = first + n // 2, half * (n % 2)
            four = attend([[nq[d + i + k, j, :, head(h)] for k in range(2)] for i in (0, 2)], j, h)
            for k in range(4):
                put(no, (h, d + k, j), four[k])
            return carry

        lax.fori_loop(0, (last - first) * 2, step, 0)

    def far(h, k):
        def step(n, carry):
            d = half * n
            j = 3 + n if k == 2 else 3 + k
            four = attend([[fq[d + i + m, k, :, head(h)] for m in range(2)] for i in (0, 2)], j, h)
            for i in range(4):
                put(fo, (h, k, d + i), four[i])
            return carry

        lax.fori_loop(0, 2, step, 0)
        relay_o[h, k, 0] = fo[h, k, 0]
        return remote(
            [(fo.at[h, k, d], relay_o.at[h, k, d], to_lane(-d)) for d in range(1, PLANE)],
            fo.at[h, k, lanes],
            relay_o.at[h, k, lanes],
        )

    returned = []

    def pass_far(h, k, copy):
        copy.wait_recv()
        columns = pl.ds(0, SLOT)
        returned.append(along(k, relay_o.at[h, k, :, :, columns], ret[h].at[5 + k, :, :, columns], -1))
        lanes_at = lax.broadcasted_iota(jnp.int32, (LEN, HD), 1)
        for n in range(2):
            tile = jnp.zeros((LEN, HD), jnp.float32)
            for i in range(half):
                tail = relay_o[h, k, n * half + i, :, SLOT:].astype(jnp.float32)
                tail = jnp.where(lanes_at < 3 * GROUP, tail, 0.0)
                tile += pltpu.roll(tail, 3 * GROUP * i, 1) if i else tail
            lse_out[h, k, n] = tile.astype(jnp.bfloat16)
        returned.append(along(k, lse_out.at[h, k], lse_in.at[h, k], -1))

    def unpack(h):
        for k in range(3):
            for n in range(2):
                tile = lse_in[h, k, n].astype(jnp.float32)
                for i in range(half):
                    tail = pltpu.roll(tile, HD - 3 * GROUP * i, 1) if i else tile
                    ret[h][5 + k, n * half + i, :, SLOT:] = tail.astype(jnp.bfloat16)

    def give_near(h, first, last):
        span = pl.ds(first, last - first)
        returned.append(remote(
            [(no.at[h, d, span], ret[h].at[span, d], to_lane(-d)) for d in range(1, PLANE)],
            no.at[h, lanes, span],
            ret[h].at[span, lanes],
        ))
        for j in range(first, last):
            ret[h][j, 0] = no[h, 0, j]

    near_y.wait_recv()
    near(0, 0, 1)
    edge0 = [relay(0, w, next0[w]) for w in range(2)]
    near(1, 0, 1)
    near(0, 1, 3)
    give_near(0, 0, 3)
    edge1 = [relay(1, w, next1[w]) for w in range(2)]
    near(1, 1, 3)
    give_near(1, 0, 3)
    far_y.wait_recv()
    for copy in edge0:
        copy.wait_recv()
    back = {k: far(0, k) for k in (2, 0, 1)}
    near(0, 3, 5)
    give_near(0, 3, 5)
    for copy in edge1:
        copy.wait_recv()
    for k in (2, 0, 1):
        pass_far(0, k, back[k])
    first = len(returned)
    back = {2: far(1, 2), 0: far(1, 0)}
    pass_far(1, 2, back[2])
    back[1] = far(1, 1)
    pass_far(1, 0, back[0])
    near(1, 3, 4)
    give_near(1, 3, 4)
    pass_far(1, 1, back[1])
    near(1, 4, 5)
    give_near(1, 4, 5)

    def write(h, n):
        span = pl.ds(n * 8, 8)
        return pltpu.make_async_copy(
            mixed.at[h, span], out.at[span, :, pl.ds(h * SLOT, SLOT)], out_sem.at[h, n]
        )

    def blend(h):
        def step(n, carry):
            for i in range(8):
                c = n * 8 + i
                distance = (prompt[c] // PLANE - z + RING) % RING
                place = jnp.where(
                    distance < 3,
                    distance + distance // 2,
                    jnp.where(distance < 6, 5 + (distance - 3) * 2 - (distance - 3) // 2 * 3, 16 - 2 * distance),
                )
                slot = ret[h][place, (prompt[c] - lane + PLANE) % PLANE]
                tail = slot[:, SLOT:].astype(jnp.float32)
                far_lse = tail[:, :GROUP] + tail[:, GROUP : 2 * GROUP] + tail[:, 2 * GROUP : 3 * GROUP]
                near_lse = own_lse[c, h][:, :GROUP]
                ceiling = jnp.maximum(far_lse, near_lse)
                a, b = jnp.exp(far_lse - ceiling), jnp.exp(near_lse - ceiling)
                a = a / (a + b)
                for g in range(GROUP):
                    part = slice(g * HD, (g + 1) * HD)
                    mine = own[c, :, h * SLOT + g * HD : h * SLOT + (g + 1) * HD]
                    theirs = slot[:, part].astype(jnp.float32)
                    mixed[h, c, :, part] = (mine + (theirs - mine) * a[:, g : g + 1]).astype(jnp.bfloat16)
            write(h, n).start()
            return carry

        lax.fori_loop(0, comps // 8, step, 0)

    for copy in returned[:first]:
        copy.wait_recv()
    unpack(0)
    blend(0)
    for copy in returned[first:]:
        copy.wait_recv()
    unpack(1)
    blend(1)
    for copy in sent:
        copy.wait_send()
    for h in range(HEADS):
        for n in range(comps // 8):
            write(h, n).wait()


def hand_over(src, dst, held, sems):
    parts, rows = held.shape[:2]
    spans = [pl.ds(n * rows, rows) for n in range(parts)]
    ins = [pltpu.make_async_copy(src.at[span], held.at[n], sems.at[0, n]) for n, span in enumerate(spans)]
    outs = [pltpu.make_async_copy(held.at[n], dst.at[span], sems.at[1, n]) for n, span in enumerate(spans)]
    for copy in ins:
        copy.start()
    for n in range(parts):
        ins[n].wait()
        outs[n].start()
    for copy in outs:
        copy.wait()


def body(queries, comp_keys, comp_values, prefix_keys, prefix_values, prompt_of):
    comps = prompt_of.shape[0]
    dp = lax.axis_index("dp")
    prompt = prompt_of[:, 0]
    slot = jnp.arange(PLANE * RING)
    place = slot // PLANE
    distance = jnp.zeros_like(place)
    for n, r in enumerate(ORDER):
        distance = jnp.where(place == n, r, distance)
    wanted = (dp // PLANE + distance) % RING * PLANE + (dp + slot) % PLANE
    named = prompt[None, :] == wanted[:, None]
    table = jnp.sum(jnp.where(named, jnp.arange(comps)[None, :], 0), axis=1).astype(jnp.int32)
    keys = prefix_keys.shape[0] * lax.axis_size("mp")
    bf16 = jnp.bfloat16
    blocks = comp_keys.shape[0] // HD
    vmem, smem = pl.BlockSpec(memory_space=pltpu.VMEM), pl.BlockSpec(memory_space=pltpu.SMEM)
    hbm = pl.BlockSpec(memory_space=pl.ANY)
    copies = 40
    out = pl.pallas_call(
        kernel,
        out_shape=jax.ShapeDtypeStruct((comps, LEN, queries.shape[1]), bf16),
        in_specs=[smem, smem, hbm, hbm, hbm, hbm, hbm],
        out_specs=hbm,
        scratch_shapes=[
            pltpu.VMEM((comps, LEN, HEADS * SLOT), bf16),
            pltpu.VMEM((blocks, HD, HEADS * HD), bf16),
            pltpu.VMEM((blocks, HD, HEADS * HD), bf16),
            pltpu.VMEM((5, HEADS, 2, keys, HD), bf16),
            pltpu.VMEM((PLANE, 5, LEN, HEADS * SLOT), bf16),
            pltpu.VMEM((3, PLANE, LEN, HEADS * SLOT), bf16),
            pltpu.VMEM((PLANE, 5, LEN, HEADS * SLOT), bf16),
            pltpu.VMEM((PLANE, 3, LEN, HEADS * SLOT), bf16),
            pltpu.VMEM((PLANE, 3, LEN, HEADS * SLOT), bf16),
            pltpu.VMEM((HEADS, PLANE, 5, LEN, WIDE), bf16),
            pltpu.VMEM((HEADS, 3, PLANE, LEN, WIDE), bf16),
            pltpu.VMEM((HEADS, 3, PLANE, LEN, WIDE), bf16),
            pltpu.VMEM((RING, PLANE, LEN, WIDE), bf16),
            pltpu.VMEM((RING, PLANE, LEN, WIDE), bf16),
            pltpu.VMEM((comps, LEN, HEADS * SLOT), jnp.float32),
            pltpu.VMEM((comps, HEADS, LEN, HD), jnp.float32),
            pltpu.VMEM((HEADS, comps, LEN, SLOT), bf16),
            pltpu.VMEM((HEADS, 3, 2, LEN, HD), bf16),
            pltpu.VMEM((HEADS, 3, 2, LEN, HD), bf16),
            pltpu.SemaphoreType.DMA((copies,)),
            pltpu.SemaphoreType.DMA((copies,)),
            pltpu.SemaphoreType.DMA((4,)),
            pltpu.SemaphoreType.DMA((3,)),
            pltpu.SemaphoreType.DMA((HEADS, comps // 8)),
        ],
        compiler_params=pltpu.CompilerParams(
            collective_id=0, has_side_effects=True, vmem_limit_bytes=60 * 1024 * 1024
        ),
        name="attend_all",
    )(
        table,
        prompt,
        queries.reshape(comps, LEN, -1),
        comp_keys.reshape(blocks, HD, -1),
        comp_values.reshape(blocks, HD, -1),
        prefix_keys,
        prefix_values,
    )
    return pl.pallas_call(
        hand_over,
        out_shape=jax.ShapeDtypeStruct(queries.shape, bf16),
        in_specs=[hbm],
        out_specs=hbm,
        scratch_shapes=[
            pltpu.VMEM((8, queries.shape[0] // 8, queries.shape[1]), bf16),
            pltpu.SemaphoreType.DMA((2, 8)),
        ],
        name="hand_over",
    )(out.reshape(queries.shape))


def solution(mesh):
    placed = (
        P("dp", "mp"),
        P("dp", "mp"),
        P("dp", "mp"),
        P(("dp", "mp"), None),
        P(("dp", "mp"), None),
        P("dp", None),
    )
    return jax.shard_map(body, mesh=mesh, in_specs=placed, out_specs=P("dp", "mp"), check_vma=False)
```
